32 devices in a mesh: grp: 2 (over y), lat: 4 (over z), lon: 2 (over x), lev: 2 (over core).
Axes of the slice: x: 2, y: 2, z: 4, core: 2. Of those that a mesh axis runs over, the one named last changes fastest.
Arguments:
- snapshot: bfloat16 [256, 128, 512], P(('grp', 'lev'), 'lat', 'lon'), parts along dimension 0, may hold values from -6 to 6
- level_factor: bfloat16 [128, 48], P('lev'), may hold values from -0.75 to 0.75
- lon_factor: bfloat16 [512, 192], P('lon'), may hold values from -0.375 to 0.375
- lat_factor: bfloat16 [128, 384], P('lat'), may hold values from -0.75 to 0.75
Outputs:
- core: float32 [96, 192, 384], P(('grp', 'lev'), 'lon', 'lat'), parts along dimension 0
The draws below stay inside these ranges and needn't reach their ends.
There are 2 independent parts, one for each index of `grp`. The reference program is written for one: setup_inputs(seed, part) draws one part's arguments, and reference() takes and returns one part's arrays. A program takes and returns all parts, laid end to end along the dimension named above; an argument that names none is the same for every part. Nothing has to cross between parts.
All inputs are finite; a program needn't handle non-finite values.
Results may differ from the reference program's by a relative error of at most 0.0003.
Values may be sent and summed in bfloat16 or wider, within the bound.
A program may use at most 64 MiB of HBM per device.

```python
import jax
import jax.numpy as jnp
from jax import lax

R1 = 384
R2 = 192
R3 = 48
NLEV = 128
NLAT = 128
NLON = 512


def with_spikes(entries, rng, source, target, parts, factor):
    def block_of(dim):
        return (jnp.arange(entries.shape[dim]) // (entries.shape[dim] // parts)).reshape((-1,) + (1,) * (entries.ndim - 1 - dim))

    near = jax.random.permutation(rng, parts)[block_of(target)]
    second = (block_of(target) + parts // 2) % parts
    return jnp.where((block_of(source) == near) | (block_of(source) == second), factor * entries, entries)


def shard_levels(own_key, dims, cuts, low, top_value):
    gain, own = 1.0, jax.random.fold_in(own_key, 6)
    for position, blocks in cuts:
        draws = jnp.exp(jax.random.uniform(jax.random.fold_in(own, position), (blocks,), jnp.float32, low / len(cuts), top_value / len(cuts)))
        gain = gain * jnp.repeat(draws, dims[position] // blocks).reshape([-1 if axis == position else 1 for axis in range(len(dims))])
    return gain


def bell_draw(stream_key, extent, deviation, bound, pieces=(), dtype=jnp.bfloat16):
    drawn = deviation * jax.random.normal(stream_key, extent, jnp.float32)
    if pieces:
        drawn = drawn * shard_levels(stream_key, extent, pieces, -0.22, 0.18)
    return jnp.clip(drawn, -bound, bound).astype(dtype)


def noise_with(stream_key, extent, deviation, reach, split, heavy, kind=jnp.bfloat16):
    result = deviation * jax.random.normal(stream_key, extent, jnp.float32)
    if split:
        result = result * shard_levels(stream_key, extent, split, -0.22, 0.18)
    return jnp.clip(with_spikes(result, jax.random.fold_in(stream_key, 3), *heavy), -reach, reach).astype(kind)


def setup_inputs(seed: int = 0, part: int = 0) -> dict:
    key_of = jax.random.split(jax.random.key(seed), 5)
    own_keys = jax.random.split(jax.random.fold_in(key_of[4], part), 5)
    snapshot = bell_draw(own_keys[0], (NLEV, NLAT, NLON), 1.0, 6.0, ((0, 2), (1, 4), (2, 2)))
    level_factor = noise_with(key_of[1], (NLEV, R3), NLEV ** -0.5, 0.75, ((0, 2),), (0, 1, 2, 2.0))
    lon_factor = noise_with(key_of[2], (NLON, R2), NLON ** -0.5, 0.375, ((0, 2),), (0, 1, 2, 2.0))
    lat_factor = noise_with(key_of[3], (NLAT, R1), NLAT ** -0.5, 0.75, ((0, 4),), (0, 1, 4, 2.0))
    return {"snapshot": snapshot, "level_factor": level_factor, "lon_factor": lon_factor, "lat_factor": lat_factor}


def reference(snapshot, level_factor, lon_factor, lat_factor):
    first = jnp.einsum('kij,kr->rij', snapshot.astype(jnp.float32), level_factor.astype(jnp.float32), precision=lax.Precision.HIGHEST)
    second = jnp.einsum('rij,js->ris', first, lon_factor.astype(jnp.float32), precision=lax.Precision.HIGHEST)
    return jnp.einsum('ris,it->rst', second, lat_factor.astype(jnp.float32), precision=lax.Precision.HIGHEST)
```

```python
import functools

import jax
import jax.numpy as jnp
from jax import lax
from jax.experimental import pallas as pl
from jax.experimental.pallas import tpu as pltpu
from jax.sharding import PartitionSpec as P

MESH = pl.DeviceIdType.MESH
F32, BF16 = jnp.float32, jnp.bfloat16
SCALE = 2.0**13
RG = 8
IB = 16


def body(snapshot, level_factor, lon_factor, lat_factor):
    first = lax.psum_scatter(
        jnp.einsum("kij,kr->rij", snapshot, level_factor, preferred_element_type=jnp.float32),
        "lev",
        scatter_dimension=0,
        tiled=True,
    )
    lon_term = jnp.einsum(
        "rij,js->ris", first, lon_factor.astype(jnp.float32), precision=lax.Precision.HIGHEST
    )
    second = lax.psum_scatter(lon_term, "lon", scatter_dimension=2, tiled=True)
    lat_term = jnp.einsum(
        "ris,it->rst", second, lat_factor.astype(jnp.float32), precision=lax.Precision.HIGHEST
    )
    return lax.psum_scatter(lat_term, "lat", scatter_dimension=2, tiled=True)


def iota(shape, dim):
    return lax.broadcasted_iota(jnp.int32, shape, dim)


def dot(a, b):
    return jnp.dot(a, b, preferred_element_type=F32)


def dot_nt(a, b):
    return lax.dot_general(a, b, (((1,), (1,)), ((), ())), preferred_element_type=F32)


def encode(v, gain):
    w = v * gain
    w2 = w * w
    w4 = w2 * w2
    w8 = w4 * w4
    return jnp.where(w < 0, -w8, w8).astype(BF16)


def decode(u, factor):
    u = u.astype(F32)
    fourth = lax.rsqrt(lax.rsqrt(jnp.maximum(jnp.abs(u), 1e-37)))
    root = fourth * lax.rsqrt(fourth) * factor
    return jnp.where(u < 0, -root, jnp.where(u > 0, root, 0.0))


def hi_lo(v):
    hi = v.astype(BF16)
    return hi, (v - hi.astype(F32)).astype(BF16)


def kernel(
    nz, x_ref, l_ref, o_ref, a_ref, out_ref,
    mx, w, f_ref, pown, psend, precv, xs, xr, g, ag, ptile, pr, mt, acc,
    d_send, d_recv, p_send, p_recv, x_send, x_recv, a_send, a_recv, m_send, m_recv, g_send, g_recv,
):
    nk, ni, nj = x_ref.shape
    nr = l_ref.shape[1]
    ns = o_ref.shape[1]
    half = nr // 2
    nq = half // RG
    sh = ns // 2
    nt = a_ref.shape[1]
    tb = nt // nz
    lanes = RG * ni
    z = lax.axis_index("lat")
    x = lax.axis_index("lon")
    c = lax.axis_index("lev")
    mates = ({"lev": 1 - c}, {"lon": 1 - x}, {"lon": 1 - x, "lev": 1 - c})
    zpeers = [lax.rem(z + d, nz) for d in range(1, nz)]

    barrier = pltpu.get_barrier_semaphore()
    for mate in mates:
        pl.semaphore_signal(barrier, inc=1, device_id=mate, device_id_type=MESH)
    for peer in zpeers:
        pl.semaphore_signal(barrier, inc=1, device_id={"lat": peer}, device_id_type=MESH)

    def remote(src, dst, ss, rs, dev):
        return pltpu.make_async_remote_copy(
            src_ref=src, dst_ref=dst, send_sem=ss, recv_sem=rs, device_id=dev, device_id_type=MESH
        )

    rows, cols = nr * IB, nk * IB
    spread_r = (iota((rows, nr), 0) // IB == iota((rows, nr), 1)).astype(BF16)
    spread_k = (iota((nk, cols), 1) // IB == iota((nk, cols), 0)).astype(BF16)
    lr = dot_nt(spread_r, l_ref[...]).astype(BF16)
    same = iota((rows, cols), 0) % IB == iota((rows, cols), 1) % IB
    mx[...] = jnp.where(same, dot(lr, spread_k), 0.0).astype(BF16)

    pl.semaphore_wait(barrier, 3 + nz - 1)
    a_copies = [
        remote(a_ref, ag.at[z], a_send.at[d], a_recv.at[z], {"lat": peer}) for d, peer in enumerate(zpeers)
    ]
    for copy in a_copies:
        copy.start()
    ag[z] = a_ref[...]

    ot = jnp.transpose(o_ref[...].astype(F32)).astype(BF16)
    most = jnp.zeros((8, 128), F32)
    d_copies = []
    for side in range(2):
        h = (1 - c) if side == 0 else c
        rws = pl.ds(pl.multiple_of(h * (half * IB), half * IB), half * IB)
        part = mx[rws, :]
        for ib in range(ni // IB):
            blk = x_ref[:, ib * IB : (ib + 1) * IB, :].reshape(nk * IB, nj)
            f_ref[:, ib] = dot(part, blk).reshape(half, IB, nj)
        for q in range(nq):
            hi, lo = hi_lo(f_ref[q * RG : (q + 1) * RG].reshape(lanes, nj))
            p = dot_nt(ot, hi) + dot_nt(ot, lo)
            m = jnp.max(jnp.abs(p).reshape(ns // 8, 8, lanes), axis=0)
            for j in range(lanes // 128):
                most = jnp.maximum(most, m[:, j * 128 : (j + 1) * 128])
            if side == 0:
                psend[q] = p
                copy = remote(psend.at[q], precv.at[q], d_send.at[q], d_recv.at[q], mates[0])
                copy.start()
                d_copies.append(copy)
            else:
                pown[q] = p
    ptile[...] = most
    p_copies = [
        remote(ptile, pr.at[n], p_send.at[n], p_recv.at[n], mate) for n, mate in enumerate(mates)
    ]
    for copy in p_copies:
        copy.start()

    w[...] = jnp.zeros(w.shape, BF16)
    for d, peer in enumerate(zpeers):
        remote(a_ref, ag.at[peer], a_send.at[d], a_recv.at[peer], {"lat": peer}).wait_recv()
    pick = iota((nt, 128), 1)
    pick = ((iota((nt, 128), 0) == pick + z * tb) & (pick < tb)).astype(BF16)
    for b in range(nz):
        mine = dot(ag[b], pick).astype(BF16)
        for r in range(RG):
            w[b, r * ni : (r + 1) * ni, r * 128 : (r + 1) * 128] = mine
    acc[...] = jnp.zeros(acc.shape, F32)

    for copy in p_copies:
        copy.wait()
    m = jnp.maximum(jnp.maximum(most, pr[0]), jnp.maximum(pr[1], pr[2]))
    m = jnp.maximum(jnp.max(jnp.max(m, axis=0, keepdims=True), axis=1, keepdims=True), 1e-30)
    mt[z] = jnp.broadcast_to(m, (8, 128))
    m_copies = [
        remote(mt.at[z], mt.at[z], m_send.at[d], m_recv.at[z], {"lat": peer}) for d, peer in enumerate(zpeers)
    ]
    for copy in m_copies:
        copy.start()
    gain, factor = SCALE / m, m * (1.0 / SCALE)

    mine = pl.ds(pl.multiple_of(x * sh, sh), sh)
    theirs = pl.ds(pl.multiple_of((1 - x) * sh, sh), sh)
    x_copies = []
    for q in range(nq):
        d_copies[q].wait_recv()
        xs[q] = encode(pown[q, theirs, :] + precv[q, theirs, :], gain)
        copy = remote(xs.at[q], xr.at[q], x_send.at[q], x_recv.at[q], mates[1])
        copy.start()
        x_copies.append(copy)

    def hop(side, d, b, q):
        to = z + 1 if side == 0 else z - 1
        return remote(g.at[b, q], g.at[b, q], g_send.at[side, d, q], g_recv.at[b, q], {"lat": to})

    def goes(side):
        return z < nz - 1 if side == 0 else z > 0

    def block(side, d):
        return z - d if side == 0 else z + d

    def exists(b):
        return (b >= 0) & (b < nz)

    for q in range(nq):
        x_copies[q].wait_recv()
        val = pown[q, mine, :] + precv[q, mine, :] + decode(xr[q], factor)
        g[z, q] = encode(val, gain)
        for side in range(2):

            @pl.when(goes(side))
            def _():
                hop(side, 0, z, q).start()

    def use(b):
        lhs = decode(g[b].reshape(nq * sh, lanes), mt[b][0:1, 0:1] * (1.0 / SCALE))
        hi, lo = hi_lo(lhs)
        acc[...] += dot(hi, w[b]) + dot(lo, w[b])

    use(z)
    for d, peer in enumerate(zpeers):
        remote(mt.at[z], mt.at[peer], m_send.at[d], m_recv.at[peer], {"lat": peer}).wait_recv()

    @pl.loop(1, nz)
    def _(d):
        for q in range(nq):
            for side in range(2):
                b = block(side, d)

                @pl.when(exists(b))
                def _():
                    hop(side, 0, b, q).wait_recv()

                    @pl.when(goes(side))
                    def _():
                        hop(side, d, b, q).start()

        @pl.loop(0, 2)
        def _(side):
            b = jnp.where(side == 0, z - d, z + d)

            @pl.when(exists(b))
            def _():
                use(b)

    for q in range(nq):
        for r in range(RG):
            out_ref[q * RG + r] = acc[q * sh : (q + 1) * sh, r * 128 : r * 128 + tb]

    for copy in a_copies + d_copies + m_copies + x_copies:
        copy.wait_send()

    @pl.loop(0, nz - 1)
    def _(d):
        for q in range(nq):
            for side in range(2):
                b = block(side, d)

                @pl.when(exists(b) & goes(side))
                def _():
                    hop(side, d, b, q).wait_send()


def fused(nz, snapshot, level_factor, lon_factor, lat_factor):
    nk, ni, nj = snapshot.shape
    nr, ns, nt = level_factor.shape[1], lon_factor.shape[1], lat_factor.shape[1]
    half, sh, tb, lanes = nr // 2, ns // 2, nt // nz, RG * ni
    nq = half // RG
    dma = lambda *shape: pltpu.SemaphoreType.DMA(shape)
    vmem = pl.BlockSpec(memory_space=pltpu.VMEM)
    return pl.pallas_call(
        functools.partial(kernel, nz),
        out_shape=jax.ShapeDtypeStruct((half, sh, tb), F32),
        in_specs=[vmem] * 4,
        out_specs=vmem,
        scratch_shapes=[
            pltpu.VMEM((nr * IB, nk * IB), BF16),
            pltpu.VMEM((nz, lanes, RG * 128), BF16),
            pltpu.VMEM((half, ni // IB, IB, nj), F32),
            pltpu.VMEM((nq, ns, lanes), F32),
            pltpu.VMEM((nq, ns, lanes), F32),
            pltpu.VMEM((nq, ns, lanes), F32),
            pltpu.VMEM((nq, sh, lanes), BF16),
            pltpu.VMEM((nq, sh, lanes), BF16),
            pltpu.VMEM((nz, nq, sh, lanes), BF16),
            pltpu.VMEM((nz, ni, nt), BF16),
            pltpu.VMEM((8, 128), F32),
            pltpu.VMEM((3, 8, 128), F32),
            pltpu.VMEM((nz, 8, 128), F32),
            pltpu.VMEM((nq * sh, RG * 128), F32),
            dma(nq), dma(nq), dma(3), dma(3), dma(nq), dma(nq),
            dma(nz - 1), dma(nz), dma(nz - 1), dma(nz), dma(2, nz, nq), dma(nz, nq),
        ],
        compiler_params=pltpu.CompilerParams(
            collective_id=0, has_side_effects=True, vmem_limit_bytes=40 * 2**20
        ),
    )(snapshot, level_factor, lon_factor, lat_factor)


def solution(mesh):
    in_specs = (P(("grp", "lev"), "lat", "lon"), P("lev", None), P("lon", None), P("lat", None))
    out_specs = P(("grp", "lev"), "lon", "lat")
    size = dict(mesh.shape)
    small = size["lev"] == 2 and size["lon"] == 2 and 1 < size["lat"] <= 4
    part = functools.partial(fused, size["lat"]) if small else body
    return jax.shard_map(part, mesh=mesh, in_specs=in_specs, out_specs=out_specs, check_vma=False)
```

```python
import functools

import jax
import jax.numpy as jnp
from jax import lax
from jax.experimental import pallas as pl
from jax.experimental.pallas import tpu as pltpu
from jax.sharding import PartitionSpec as P

MESH = pl.DeviceIdType.MESH
F32, BF16 = jnp.float32, jnp.bfloat16
TOP = 2.0**7
KNEE = 2.0**-6
RG = 8
IB = 16


def body(snapshot, level_factor, lon_factor, lat_factor):
    first = lax.psum_scatter(
        jnp.einsum("kij,kr->rij", snapshot, level_factor, preferred_element_type=jnp.float32),
        "lev",
        scatter_dimension=0,
        tiled=True,
    )
    lon_term = jnp.einsum(
        "rij,js->ris", first, lon_factor.astype(jnp.float32), precision=lax.Precision.HIGHEST
    )
    second = lax.psum_scatter(lon_term, "lon", scatter_dimension=2, tiled=True)
    lat_term = jnp.einsum(
        "ris,it->rst", second, lat_factor.astype(jnp.float32), precision=lax.Precision.HIGHEST
    )
    return lax.psum_scatter(lat_term, "lat", scatter_dimension=2, tiled=True)


def iota(shape, dim):
    return lax.broadcasted_iota(jnp.int32, shape, dim)


def dot(a, b):
    return jnp.dot(a, b, preferred_element_type=F32)


def dot_nt(a, b):
    return lax.dot_general(a, b, (((1,), (1,)), ((), ())), preferred_element_type=F32)


def encode(v, gain):
    w = v * gain
    small = jnp.abs(w) < KNEE
    w2 = w * w
    w4 = w2 * w2
    w8 = w4 * w4
    w16 = w8 * w8
    return jnp.where(small, w * (KNEE**15), jnp.where(w < 0, -w16, w16)).astype(BF16)


def decode(u, factor):
    u = u.astype(F32)
    size = jnp.abs(u)
    root = jnp.maximum(size, KNEE**16)
    root = lax.rsqrt(lax.rsqrt(root))
    root = lax.rsqrt(lax.rsqrt(root))
    return jnp.where(size < KNEE**16, u * (KNEE**-15), jnp.where(u < 0, -root, root)) * factor


def hi_lo(v):
    hi = v.astype(BF16)
    return hi, (v - hi.astype(F32)).astype(BF16)


def kernel(
    nz, x_hbm, l_hbm, o_hbm, a_hbm, out_ref,
    x_ref, l_ref, o_ref, in_sem, mx, w, f_ref, pown, psend, precv, xs, xr, g, ag, ptile, pr, mt, acc,
    d_send, d_recv, p_send, p_recv, x_send, x_recv, a_send, a_recv, m_send, m_recv, g_send, g_recv,
):
    nk, ni, nj = x_ref.shape
    nr = l_ref.shape[0]
    ns = o_ref.shape[0]
    half = nr // 2
    nq = half // RG
    sh = ns // 2
    nt = a_hbm.shape[1]
    tb = nt // nz
    lanes = RG * ni
    z = lax.axis_index("lat")
    x = lax.axis_index("lon")
    c = lax.axis_index("lev")
    mates = ({"lev": 1 - c}, {"lon": 1 - x}, {"lon": 1 - x, "lev": 1 - c})
    zpeers = [lax.rem(z + d, nz) for d in range(1, nz)]

    loads = [
        pltpu.make_async_copy(src, dst, in_sem.at[n])
        for n, (src, dst) in enumerate(((l_hbm, l_ref), (a_hbm, ag.at[z]), (x_hbm, x_ref), (o_hbm, o_ref)))
    ]
    for load in loads:
        load.start()
    barrier = pltpu.get_barrier_semaphore()
    for mate in mates:
        pl.semaphore_signal(barrier, inc=1, device_id=mate, device_id_type=MESH)
    for peer in zpeers:
        pl.semaphore_signal(barrier, inc=1, device_id={"lat": peer}, device_id_type=MESH)

    def remote(src, dst, ss, rs, dev):
        return pltpu.make_async_remote_copy(
            src_ref=src, dst_ref=dst, send_sem=ss, recv_sem=rs, device_id=dev, device_id_type=MESH
        )

    rows, cols = nr * IB, nk * IB
    spread_r = (iota((rows, nr), 0) // IB == iota((rows, nr), 1)).astype(BF16)
    spread_k = (iota((nk, cols), 1) // IB == iota((nk, cols), 0)).astype(BF16)
    same = (iota((IB, 128), 0) == iota((IB, 128), 1) % IB).astype(F32)
    loads[0].wait()
    lr = dot(spread_r, l_ref[...]).astype(BF16)
    for j in range(cols // 128):
        spread = dot(lr, spread_k[:, j * 128 : (j + 1) * 128]).reshape(nr, IB, 128) * same
        mx[:, j * 128 : (j + 1) * 128] = spread.reshape(rows, 128).astype(BF16)

    loads[1].wait()
    pl.semaphore_wait(barrier, 3 + nz - 1)
    a_copies = [
        remote(ag.at[z], ag.at[z], a_send.at[d], a_recv.at[z], {"lat": peer}) for d, peer in enumerate(zpeers)
    ]
    for copy in a_copies:
        copy.start()
    loads[2].wait()
    loads[3].wait()
    most = jnp.zeros((8, 128), F32)
    d_copies = []
    for side in range(2):
        h = (1 - c) if side == 0 else c
        rws = pl.ds(pl.multiple_of(h * (half * IB), half * IB), half * IB)
        part = mx[rws, :]
        for ib in range(ni // IB):
            blk = x_ref[:, ib * IB : (ib + 1) * IB, :].reshape(nk * IB, nj)
            f_ref[:, ib] = dot(part, blk).reshape(half, IB, nj)
        for q in range(nq):
            hi, lo = hi_lo(f_ref[q * RG : (q + 1) * RG].reshape(lanes, nj))
            p = dot_nt(o_ref[...], hi) + dot_nt(o_ref[...], lo)
            m = jnp.max(jnp.abs(p).reshape(ns // 8, 8, lanes), axis=0)
            for j in range(lanes // 128):
                most = jnp.maximum(most, m[:, j * 128 : (j + 1) * 128])
            if side == 0:
                psend[q] = p
                copy = remote(psend.at[q], precv.at[q], d_send.at[q], d_recv.at[q], mates[0])
                copy.start()
                d_copies.append(copy)
            else:
                pown[q] = p
    ptile[...] = most
    p_copies = [
        remote(ptile, pr.at[n], p_send.at[n], p_recv.at[n], mate) for n, mate in enumerate(mates)
    ]
    for copy in p_copies:
        copy.start()

    w[...] = jnp.zeros(w.shape, BF16)
    for d, peer in enumerate(zpeers):
        remote(ag.at[z], ag.at[peer], a_send.at[d], a_recv.at[peer], {"lat": peer}).wait_recv()
    pick = iota((nt, 128), 1)
    pick = ((iota((nt, 128), 0) == pick + z * tb) & (pick < tb)).astype(BF16)
    for b in range(nz):
        mine = dot(ag[b], pick).astype(BF16)
        for r in range(RG):
            w[b, r * ni : (r + 1) * ni, r * 128 : (r + 1) * 128] = mine
    acc[...] = jnp.zeros(acc.shape, F32)

    for copy in p_copies:
        copy.wait()
    m = jnp.maximum(jnp.maximum(most, pr[0]), jnp.maximum(pr[1], pr[2]))
    m = jnp.maximum(jnp.max(jnp.max(m, axis=0, keepdims=True), axis=1, keepdims=True), 1e-30)
    mt[z] = jnp.broadcast_to(m, (8, 128))
    m_copies = [
        remote(mt.at[z], mt.at[z], m_send.at[d], m_recv.at[z], {"lat": peer}) for d, peer in enumerate(zpeers)
    ]
    for copy in m_copies:
        copy.start()
    gain, factor = (TOP / 4) / m, m * (4 / TOP)

    mine = pl.ds(pl.multiple_of(x * sh, sh), sh)
    theirs = pl.ds(pl.multiple_of((1 - x) * sh, sh), sh)
    x_copies = []
    for q in range(nq):
        d_copies[q].wait_recv()
        xs[q] = encode(pown[q, theirs, :] + precv[q, theirs, :], gain)
        copy = remote(xs.at[q], xr.at[q], x_send.at[q], x_recv.at[q], mates[1])
        copy.start()
        x_copies.append(copy)

    def hop(side, d, b, q):
        to = z + 1 if side == 0 else z - 1
        return remote(g.at[b, q], g.at[b, q], g_send.at[side, d, q], g_recv.at[b, q], {"lat": to})

    def goes(side):
        return z < nz - 1 if side == 0 else z > 0

    def block(side, d):
        return z - d if side == 0 else z + d

    def exists(b):
        return (b >= 0) & (b < nz)

    for q in range(nq):
        x_copies[q].wait_recv()
        val = pown[q, mine, :] + precv[q, mine, :] + decode(xr[q], factor)
        g[z, q] = encode(val, gain)
        for side in range(2):

            @pl.when(goes(side))
            def _():
                hop(side, 0, z, q).start()

    def use(b, q):
        hi, lo = hi_lo(decode(g[b, q], mt[b][0:1, 0:1] * (4 / TOP)))
        both = dot(jnp.concatenate([hi, lo], axis=0), w[b])
        acc[q] += both[:sh] + both[sh:]

    for q in range(nq):
        use(z, q)
    for d, peer in enumerate(zpeers):
        remote(mt.at[z], mt.at[peer], m_send.at[d], m_recv.at[peer], {"lat": peer}).wait_recv()

    @pl.loop(1, nz)
    def _(d):
        for q in range(nq):
            for side in range(2):
                b = block(side, d)

                @pl.when(exists(b))
                def _():
                    hop(side, 0, b, q).wait_recv()

                    @pl.when(goes(side))
                    def _():
                        hop(side, d, b, q).start()

        @pl.loop(0, nq)
        def _(q):
            for side in range(2):
                b = block(side, d)

                @pl.when(exists(b))
                def _():
                    use(b, q)

    for q in range(nq):
        for r in range(RG):
            out_ref[q * RG + r] = acc[q, :, r * 128 : r * 128 + tb]

    for copy in a_copies + d_copies + m_copies + x_copies:
        copy.wait_send()

    @pl.loop(0, nz - 1)
    def _(d):
        for q in range(nq):
            for side in range(2):
                b = block(side, d)

                @pl.when(exists(b) & goes(side))
                def _():
                    hop(side, d, b, q).wait_send()


def fused(nz, snapshot, level_factor, lon_factor, lat_factor):
    nk, ni, nj = snapshot.shape
    nr, ns, nt = level_factor.shape[1], lon_factor.shape[1], lat_factor.shape[1]
    half, sh, tb, lanes = nr // 2, ns // 2, nt // nz, RG * ni
    nq = half // RG
    dma = lambda *shape: pltpu.SemaphoreType.DMA(shape)
    vmem = pl.BlockSpec(memory_space=pltpu.VMEM)
    return pl.pallas_call(
        functools.partial(kernel, nz),
        out_shape=jax.ShapeDtypeStruct((half, sh, tb), F32),
        in_specs=[pl.BlockSpec(memory_space=pltpu.HBM)] * 4,
        out_specs=vmem,
        scratch_shapes=[
            pltpu.VMEM((nk, ni, nj), BF16),
            pltpu.VMEM((nr, nk), BF16),
            pltpu.VMEM((ns, nj), BF16),
            dma(4),
            pltpu.VMEM((nr * IB, nk * IB), BF16),
            pltpu.VMEM((nz, lanes, RG * 128), BF16),
            pltpu.VMEM((half, ni // IB, IB, nj), F32),
            pltpu.VMEM((nq, ns, lanes), F32),
            pltpu.VMEM((nq, ns, lanes), F32),
            pltpu.VMEM((nq, ns, lanes), F32),
            pltpu.VMEM((nq, sh, lanes), BF16),
            pltpu.VMEM((nq, sh, lanes), BF16),
            pltpu.VMEM((nz, nq, sh, lanes), BF16),
            pltpu.VMEM((nz, ni, nt), BF16),
            pltpu.VMEM((8, 128), F32),
            pltpu.VMEM((3, 8, 128), F32),
            pltpu.VMEM((nz, 8, 128), F32),
            pltpu.VMEM((nq, sh, RG * 128), F32),
            dma(nq), dma(nq), dma(3), dma(3), dma(nq), dma(nq),
            dma(nz - 1), dma(nz), dma(nz - 1), dma(nz), dma(2, nz, nq), dma(nz, nq),
        ],
        compiler_params=pltpu.CompilerParams(
            collective_id=0, has_side_effects=True, vmem_limit_bytes=63 * 2**20
        ),
    )(snapshot, level_factor.T, lon_factor.T, lat_factor)


def solution(mesh):
    in_specs = (P(("grp", "lev"), "lat", "lon"), P("lev", None), P("lon", None), P("lat", None))
    out_specs = P(("grp", "lev"), "lon", "lat")
    size = dict(mesh.shape)
    small = size["lev"] == 2 and size["lon"] == 2 and 1 < size["lat"] <= 4
    part = functools.partial(fused, size["lat"]) if small else body
    return jax.shard_map(part, mesh=mesh, in_specs=in_specs, out_specs=out_specs, check_vma=False)
```

```python
import functools

import jax
import jax.numpy as jnp
from jax import lax
from jax.experimental import pallas as pl
from jax.experimental.pallas import tpu as pltpu
from jax.sharding import PartitionSpec as P

MESH = pl.DeviceIdType.MESH
F32, BF16 = jnp.float32, jnp.bfloat16
TOP = 2.0**7
KNEE = 2.0**-6
RG = 8
IB = 16


def body(snapshot, level_factor, lon_factor, lat_factor):
    first = lax.psum_scatter(
        jnp.einsum("kij,kr->rij", snapshot, level_factor, preferred_element_type=jnp.float32),
        "lev",
        scatter_dimension=0,
        tiled=True,
    )
    lon_term = jnp.einsum(
        "rij,js->ris", first, lon_factor.astype(jnp.float32), precision=lax.Precision.HIGHEST
    )
    second = lax.psum_scatter(lon_term, "lon", scatter_dimension=2, tiled=True)
    lat_term = jnp.einsum(
        "ris,it->rst", second, lat_factor.astype(jnp.float32), precision=lax.Precision.HIGHEST
    )
    return lax.psum_scatter(lat_term, "lat", scatter_dimension=2, tiled=True)


def iota(shape, dim):
    return lax.broadcasted_iota(jnp.int32, shape, dim)


def dot(a, b):
    return jnp.dot(a, b, preferred_element_type=F32)


def dot_nt(a, b):
    return lax.dot_general(a, b, (((1,), (1,)), ((), ())), preferred_element_type=F32)


def encode(v, gain):
    w = v * gain
    small = jnp.abs(w) < KNEE
    w2 = w * w
    w4 = w2 * w2
    w8 = w4 * w4
    w16 = w8 * w8
    return jnp.where(small, w * (KNEE**15), jnp.where(w < 0, -w16, w16)).astype(BF16)


def decode(u, factor):
    u = u.astype(F32)
    size = jnp.abs(u)
    root = jnp.maximum(size, KNEE**16)
    root = lax.rsqrt(lax.rsqrt(root))
    root = lax.rsqrt(lax.rsqrt(root))
    return jnp.where(size < KNEE**16, u * (KNEE**-15), jnp.where(u < 0, -root, root)) * factor


def hi_lo(v):
    hi = v.astype(BF16)
    return hi, (v - hi.astype(F32)).astype(BF16)


def kernel(
    nz, x_hbm, l_hbm, o_hbm, a_hbm, out_ref,
    x_ref, l_ref, o_ref, in_sem, mx, w, f_ref, pown, psend, precv, xs, xr, g, ag, ptile, pr, mt, acc,
    d_send, d_recv, p_send, p_recv, x_send, x_recv, a_send, a_recv, m_send, m_recv, g_send, g_recv,
):
    nk, ni, nj = x_ref.shape
    nr = l_ref.shape[0]
    ns = o_ref.shape[0]
    half = nr // 2
    nq = half // RG
    sh = ns // 2
    nt = a_hbm.shape[1]
    tb = nt // nz
    lanes = RG * ni
    z = lax.axis_index("lat")
    x = lax.axis_index("lon")
    c = lax.axis_index("lev")
    mates = ({"lev": 1 - c}, {"lon": 1 - x})
    zpeers = [lax.rem(z + d, nz) for d in range(1, nz)]

    loads = [
        pltpu.make_async_copy(src, dst, in_sem.at[n])
        for n, (src, dst) in enumerate(((l_hbm, l_ref), (a_hbm, ag.at[z]), (x_hbm, x_ref), (o_hbm, o_ref)))
    ]
    for load in loads:
        load.start()
    barrier = pltpu.get_barrier_semaphore()
    for mate in mates:
        pl.semaphore_signal(barrier, inc=1, device_id=mate, device_id_type=MESH)
    for peer in zpeers:
        pl.semaphore_signal(barrier, inc=1, device_id={"lat": peer}, device_id_type=MESH)

    def remote(src, dst, ss, rs, dev):
        return pltpu.make_async_remote_copy(
            src_ref=src, dst_ref=dst, send_sem=ss, recv_sem=rs, device_id=dev, device_id_type=MESH
        )

    rows, cols = nr * IB, nk * IB
    spread_r = (iota((rows, nr), 0) // IB == iota((rows, nr), 1)).astype(BF16)
    spread_k = (iota((nk, cols), 1) // IB == iota((nk, cols), 0)).astype(BF16)
    same = (iota((IB, 128), 0) == iota((IB, 128), 1) % IB).astype(F32)
    loads[0].wait()
    lr = dot(spread_r, l_ref[...]).astype(BF16)
    for j in range(cols // 128):
        spread = dot(lr, spread_k[:, j * 128 : (j + 1) * 128]).reshape(nr, IB, 128) * same
        mx[:, j * 128 : (j + 1) * 128] = spread.reshape(rows, 128).astype(BF16)

    loads[1].wait()
    pl.semaphore_wait(barrier, 2 + nz - 1)
    a_copies = [
        remote(ag.at[z], ag.at[z], a_send.at[d], a_recv.at[z], {"lat": peer}) for d, peer in enumerate(zpeers)
    ]
    for copy in a_copies:
        copy.start()
    loads[2].wait()
    loads[3].wait()
    d_copies = []
    for side in range(2):
        h = (1 - c) if side == 0 else c
        rws = pl.ds(pl.multiple_of(h * (half * IB), half * IB), half * IB)
        part = mx[rws, :]
        for ib in range(ni // IB):
            blk = x_ref[:, ib * IB : (ib + 1) * IB, :].reshape(nk * IB, nj)
            f_ref[:, ib] = dot(part, blk).reshape(half, IB, nj)
        for q in range(nq):
            hi, lo = hi_lo(f_ref[q * RG : (q + 1) * RG].reshape(lanes, nj))
            p = dot_nt(o_ref[...], hi) + dot_nt(o_ref[...], lo)
            if side == 0:
                psend[q] = p
                copy = remote(psend.at[q], precv.at[q], d_send.at[q], d_recv.at[q], mates[0])
                copy.start()
                d_copies.append(copy)
            else:
                pown[q] = p
    most = jnp.zeros((8, 128), F32)
    for q in range(nq):
        d_copies[q].wait_recv()
        pown[q] = pown[q] + precv[q]
        m = jnp.max(jnp.abs(pown[q]).reshape(ns // 8, 8, lanes), axis=0)
        for j in range(lanes // 128):
            most = jnp.maximum(most, m[:, j * 128 : (j + 1) * 128])
    m_own = jnp.max(jnp.max(most, axis=0, keepdims=True), axis=1, keepdims=True)
    m_own = jnp.maximum(m_own, 1e-30)
    gain = TOP / m_own
    ptile[...] = jnp.broadcast_to(m_own, (8, 128))
    p_copy = remote(ptile, pr, p_send, p_recv, mates[1])
    p_copy.start()
    mine = pl.ds(pl.multiple_of(x * sh, sh), sh)
    theirs = pl.ds(pl.multiple_of((1 - x) * sh, sh), sh)
    x_copies = []
    for q in range(nq):
        xs[q] = encode(pown[q, theirs, :], gain)
        copy = remote(xs.at[q], xr.at[q], x_send.at[q], x_recv.at[q], mates[1])
        copy.start()
        x_copies.append(copy)

    w[...] = jnp.zeros(w.shape, BF16)
    for d, peer in enumerate(zpeers):
        remote(ag.at[z], ag.at[peer], a_send.at[d], a_recv.at[peer], {"lat": peer}).wait_recv()
    pick = iota((nt, 128), 1)
    pick = ((iota((nt, 128), 0) == pick + z * tb) & (pick < tb)).astype(BF16)
    for b in range(nz):
        own_t = dot(ag[b], pick).astype(BF16)
        for r in range(RG):
            w[b, r * ni : (r + 1) * ni, r * 128 : (r + 1) * 128] = own_t

    p_copy.wait()
    m_x = pr[0:1, 0:1]
    m = m_own + m_x
    mt[z] = jnp.broadcast_to(m, (8, 128))
    m_copies = [
        remote(mt.at[z], mt.at[z], m_send.at[d], m_recv.at[z], {"lat": peer}) for d, peer in enumerate(zpeers)
    ]
    for copy in m_copies:
        copy.start()
    gain, factor = TOP / m, m_x * (1 / TOP)

    def hop(side, d, b, q):
        to = z + 1 if side == 0 else z - 1
        return remote(g.at[b, q], g.at[b, q], g_send.at[side, d, q], g_recv.at[b, q], {"lat": to})

    def goes(side):
        return z < nz - 1 if side == 0 else z > 0

    def block(side, d):
        return z - d if side == 0 else z + d

    def exists(b):
        return (b >= 0) & (b < nz)

    for q in range(nq):
        x_copies[q].wait_recv()
        val = pown[q, mine, :] + decode(xr[q], factor)
        g[z, q] = encode(val, gain)
        for side in range(2):

            @pl.when(goes(side))
            def _():
                hop(side, 0, z, q).start()

    def use(b, q, own=False):
        hi, lo = hi_lo(decode(g[b, q], mt[b][0:1, 0:1] * (1 / TOP)))
        both = dot(jnp.concatenate([hi, lo], axis=0), w[b])
        acc[q] = both[:sh] + both[sh:] + (0.0 if own else acc[q])

    for q in range(nq):
        use(z, q, own=True)
    for d, peer in enumerate(zpeers):
        remote(mt.at[z], mt.at[peer], m_send.at[d], m_recv.at[peer], {"lat": peer}).wait_recv()

    @pl.loop(1, nz)
    def _(d):
        for q in range(nq):
            for side in range(2):
                b = block(side, d)

                @pl.when(exists(b))
                def _():
                    hop(side, 0, b, q).wait_recv()

                    @pl.when(goes(side))
                    def _():
                        hop(side, d, b, q).start()

        @pl.loop(0, nq)
        def _(q):
            for side in range(2):
                b = block(side, d)

                @pl.when(exists(b))
                def _():
                    use(b, q)

    for q in range(nq):
        for r in range(RG):
            out_ref[q * RG + r] = acc[q, :, r * 128 : r * 128 + tb]

    for copy in a_copies + d_copies + m_copies + x_copies:
        copy.wait_send()

    @pl.loop(0, nz - 1)
    def _(d):
        for q in range(nq):
            for side in range(2):
                b = block(side, d)

                @pl.when(exists(b) & goes(side))
                def _():
                    hop(side, d, b, q).wait_send()


def fused(nz, snapshot, level_factor, lon_factor, lat_factor):
    nk, ni, nj = snapshot.shape
    nr, ns, nt = level_factor.shape[1], lon_factor.shape[1], lat_factor.shape[1]
    half, sh, tb, lanes = nr // 2, ns // 2, nt // nz, RG * ni
    nq = half // RG
    dma = lambda *shape: pltpu.SemaphoreType.DMA(shape)
    vmem = pl.BlockSpec(memory_space=pltpu.VMEM)
    return pl.pallas_call(
        functools.partial(kernel, nz),
        out_shape=pltpu.VMEM((half, sh, tb), F32),
        in_specs=[pl.BlockSpec(memory_space=pltpu.HBM)] * 4,
        out_specs=vmem,
        scratch_shapes=[
            pltpu.VMEM((nk, ni, nj), BF16),
            pltpu.VMEM((nr, nk), BF16),
            pltpu.VMEM((ns, nj), BF16),
            dma(4),
            pltpu.VMEM((nr * IB, nk * IB), BF16),
            pltpu.VMEM((nz, lanes, RG * 128), BF16),
            pltpu.VMEM((half, ni // IB, IB, nj), F32),
            pltpu.VMEM((nq, ns, lanes), F32),
            pltpu.VMEM((nq, ns, lanes), F32),
            pltpu.VMEM((nq, ns, lanes), F32),
            pltpu.VMEM((nq, sh, lanes), BF16),
            pltpu.VMEM((nq, sh, lanes), BF16),
            pltpu.VMEM((nz, nq, sh, lanes), BF16),
            pltpu.VMEM((nz, ni, nt), BF16),
            pltpu.VMEM((8, 128), F32),
            pltpu.VMEM((8, 128), F32),
            pltpu.VMEM((nz, 8, 128), F32),
            pltpu.VMEM((nq, sh, RG * 128), F32),
            dma(nq), dma(nq), pltpu.SemaphoreType.DMA, pltpu.SemaphoreType.DMA, dma(nq), dma(nq),
            dma(nz - 1), dma(nz), dma(nz - 1), dma(nz), dma(2, nz, nq), dma(nz, nq),
        ],
        compiler_params=pltpu.CompilerParams(
            collective_id=0, has_side_effects=True, vmem_limit_bytes=58 * 2**20
        ),
    )(snapshot, level_factor.T, lon_factor.T, lat_factor)


def solution(mesh):
    in_specs = (P(("grp", "lev"), "lat", "lon"), P("lev", None), P("lon", None), P("lat", None))
    out_specs = P(("grp", "lev"), "lon", "lat")
    size = dict(mesh.shape)
    small = size["lev"] == 2 and size["lon"] == 2 and 1 < size["lat"] <= 4
    part = functools.partial(fused, size["lat"]) if small else body
    return jax.shard_map(part, mesh=mesh, in_specs=in_specs, out_specs=out_specs, check_vma=False)
```

```python
import functools

import jax
import jax.numpy as jnp
from jax import lax
from jax.experimental import pallas as pl
from jax.experimental.pallas import tpu as pltpu
from jax.sharding import PartitionSpec as P

MESH = pl.DeviceIdType.MESH
F32, BF16 = jnp.float32, jnp.bfloat16
TOP = 2.0**7
KNEE = 2.0**-6
RG = 8
IB = 16


def body(snapshot, level_factor, lon_factor, lat_factor):
    first = lax.psum_scatter(
        jnp.einsum("kij,kr->rij", snapshot, level_factor, preferred_element_type=jnp.float32),
        "lev",
        scatter_dimension=0,
        tiled=True,
    )
    lon_term = jnp.einsum(
        "rij,js->ris", first, lon_factor.astype(jnp.float32), precision=lax.Precision.HIGHEST
    )
    second = lax.psum_scatter(lon_term, "lon", scatter_dimension=2, tiled=True)
    lat_term = jnp.einsum(
        "ris,it->rst", second, lat_factor.astype(jnp.float32), precision=lax.Precision.HIGHEST
    )
    return lax.psum_scatter(lat_term, "lat", scatter_dimension=2, tiled=True)


def iota(shape, dim):
    return lax.broadcasted_iota(jnp.int32, shape, dim)


def dot(a, b):
    return jnp.dot(a, b, preferred_element_type=F32)


def dot_nt(a, b):
    return lax.dot_general(a, b, (((1,), (1,)), ((), ())), preferred_element_type=F32)


def encode(v, gain):
    w = v * gain
    small = jnp.abs(w) < KNEE
    w2 = w * w
    w4 = w2 * w2
    w8 = w4 * w4
    w16 = w8 * w8
    return jnp.where(small, w * (KNEE**15), jnp.where(w < 0, -w16, w16)).astype(BF16)


def decode(u, factor):
    u = u.astype(F32)
    size = jnp.abs(u)
    root = jnp.maximum(size, KNEE**16)
    root = lax.rsqrt(lax.rsqrt(root))
    root = lax.rsqrt(lax.rsqrt(root))
    return jnp.where(size < KNEE**16, u * (KNEE**-15), jnp.where(u < 0, -root, root)) * factor


def hi_lo(v):
    hi = v.astype(BF16)
    return hi, (v - hi.astype(F32)).astype(BF16)


def kernel(
    nz, x_hbm, l_hbm, o_hbm, a_hbm, out_ref,
    x_ref, l_ref, o_ref, in_sem, mx, w, f_ref, pown, psend, precv, xs, xr, g, ag, ptile, pr, mt, acc,
    d_send, d_recv, p_send, p_recv, x_send, x_recv, a_send, a_recv, m_send, m_recv, g_send, g_recv,
):
    nk, ni, nj = x_ref.shape
    nr = l_ref.shape[0]
    ns = o_ref.shape[0]
    half = nr // 2
    nq = half // RG
    sh = ns // 2
    nt = a_hbm.shape[1]
    tb = nt // nz
    lanes = RG * ni
    z = lax.axis_index("lat")
    x = lax.axis_index("lon")
    c = lax.axis_index("lev")
    mates = ({"lev": 1 - c}, {"lon": 1 - x})
    zpeers = [lax.rem(z + d, nz) for d in range(1, nz)]

    loads = [
        pltpu.make_async_copy(src, dst, in_sem.at[n])
        for n, (src, dst) in enumerate(((l_hbm, l_ref), (a_hbm, ag.at[z]), (x_hbm, x_ref), (o_hbm, o_ref)))
    ]
    for load in loads:
        load.start()
    barrier = pltpu.get_barrier_semaphore()
    for mate in mates:
        pl.semaphore_signal(barrier, inc=1, device_id=mate, device_id_type=MESH)
    for peer in zpeers:
        pl.semaphore_signal(barrier, inc=1, device_id={"lat": peer}, device_id_type=MESH)

    def remote(src, dst, ss, rs, dev):
        return pltpu.make_async_remote_copy(
            src_ref=src, dst_ref=dst, send_sem=ss, recv_sem=rs, device_id=dev, device_id_type=MESH
        )

    rows, cols = nr * IB, nk * IB
    spread_r = (iota((rows, nr), 0) // IB == iota((rows, nr), 1)).astype(BF16)
    spread_k = (iota((nk, cols), 1) // IB == iota((nk, cols), 0)).astype(BF16)
    same = (iota((IB, 128), 0) == iota((IB, 128), 1) % IB).astype(F32)
    loads[0].wait()
    lr = dot(spread_r, l_ref[...]).astype(BF16)
    for j in range(cols // 128):
        spread = dot(lr, spread_k[:, j * 128 : (j + 1) * 128]).reshape(nr, IB, 128) * same
        mx[:, j * 128 : (j + 1) * 128] = spread.reshape(rows, 128).astype(BF16)

    loads[1].wait()
    pl.semaphore_wait(barrier, 2 + nz - 1)
    a_copies = [
        remote(ag.at[z], ag.at[z], a_send.at[d], a_recv.at[z], {"lat": peer}) for d, peer in enumerate(zpeers)
    ]
    for copy in a_copies:
        copy.start()
    loads[2].wait()
    loads[3].wait()
    d_copies = []
    for side in range(2):
        h = (1 - c) if side == 0 else c
        rws = pl.ds(pl.multiple_of(h * (half * IB), half * IB), half * IB)
        part = mx[rws, :]
        for ib in range(ni // IB):
            blk = x_ref[:, ib * IB : (ib + 1) * IB, :].reshape(nk * IB, nj)
            f_ref[:, ib] = dot(part, blk).reshape(half, IB, nj)
        for q in range(nq):
            hi, lo = hi_lo(f_ref[q * RG : (q + 1) * RG].reshape(lanes, nj))
            p = dot_nt(o_ref[...], hi) + dot_nt(o_ref[...], lo)
            if side == 0:
                psend[q] = p
                copy = remote(psend.at[q], precv.at[q], d_send.at[q], d_recv.at[q], mates[0])
                copy.start()
                d_copies.append(copy)
            else:
                pown[q] = p
    most = jnp.zeros((8, 128), F32)
    for q in range(nq):
        d_copies[q].wait_recv()
        pown[q] = pown[q] + precv[q]
        m = jnp.max(jnp.abs(pown[q]).reshape(ns // 8, 8, lanes), axis=0)
        for j in range(lanes // 128):
            most = jnp.maximum(most, m[:, j * 128 : (j + 1) * 128])
    m_own = jnp.max(jnp.max(most, axis=0, keepdims=True), axis=1, keepdims=True)
    m_own = jnp.maximum(m_own, 1e-30)
    gain = TOP / m_own
    ptile[...] = jnp.broadcast_to(m_own, (8, 128))
    p_copy = remote(ptile, pr, p_send, p_recv, mates[1])
    p_copy.start()
    mine = pl.ds(pl.multiple_of(x * sh, sh), sh)
    theirs = pl.ds(pl.multiple_of((1 - x) * sh, sh), sh)
    x_copies = []
    for q in range(nq):
        xs[q] = encode(pown[q, theirs, :], gain)
        copy = remote(xs.at[q], xr.at[q], x_send.at[q], x_recv.at[q], mates[1])
        copy.start()
        x_copies.append(copy)

    w[...] = jnp.zeros(w.shape, BF16)
    for d, peer in enumerate(zpeers):
        remote(ag.at[z], ag.at[peer], a_send.at[d], a_recv.at[peer], {"lat": peer}).wait_recv()
    pick = iota((nt, 128), 1)
    pick = ((iota((nt, 128), 0) == pick + z * tb) & (pick < tb)).astype(BF16)
    for b in range(nz):
        own_t = dot(ag[b], pick).astype(BF16)
        for r in range(RG):
            w[b, r * ni : (r + 1) * ni, r * 128 : (r + 1) * 128] = own_t

    p_copy.wait()
    m_x = pr[0:1, 0:1]
    m = m_own + m_x
    mt[z] = jnp.broadcast_to(m, (8, 128))
    m_copies = [
        remote(mt.at[z], mt.at[z], m_send.at[d], m_recv.at[z], {"lat": peer}) for d, peer in enumerate(zpeers)
    ]
    for copy in m_copies:
        copy.start()
    gain, factor = TOP / m, m_x * (1 / TOP)

    def away(side, d):
        return z + d if side == 0 else z - d

    def exists(b):
        return (b >= 0) & (b < nz)

    def send(side, d, q):
        to = away(side, d)
        return remote(g.at[z, q], g.at[z, q], g_send.at[side, d - 1, q], g_recv.at[z, q], {"lat": to})

    def forward(side, q):
        b, to = away(1 - side, 2), away(side, 1)
        return remote(g.at[b, q], g.at[b, q], g_send.at[side, 2, q], g_recv.at[b, q], {"lat": to})

    def forwards(side):
        return exists(away(1 - side, 2)) & exists(away(side, 1))

    def arrival(b, q):
        return remote(g.at[z, q], g.at[b, q], g_send.at[0, 0, q], g_recv.at[b, q], {"lat": zpeers[0]})

    for q in range(nq):
        x_copies[q].wait_recv()
        val = pown[q, mine, :] + decode(xr[q], factor)
        g[z, q] = encode(val, gain)
        for d in (2, 1):
            for side in range(2):

                @pl.when(exists(away(side, d)))
                def _():
                    send(side, d, q).start()

    def use(b, q, own=False):
        hi, lo = hi_lo(decode(g[b, q], mt[b][0:1, 0:1] * (1 / TOP)))
        both = dot(jnp.concatenate([hi, lo], axis=0), w[b])
        acc[q] = both[:sh] + both[sh:] + (0.0 if own else acc[q])

    for q in range(nq):
        use(z, q, own=True)
    for d, peer in enumerate(zpeers):
        remote(mt.at[z], mt.at[peer], m_send.at[d], m_recv.at[peer], {"lat": peer}).wait_recv()

    for q in range(nq):
        for side in range(2):

            @pl.when(exists(away(1 - side, 2)))
            def _():
                arrival(away(1 - side, 2), q).wait_recv()

                @pl.when(forwards(side))
                def _():
                    forward(side, q).start()

    for d in range(1, nz):

        @pl.loop(0, nq)
        def _(q):
            for side in range(2):
                b = away(side, d)

                @pl.when(exists(b))
                def _():
                    if d != 2:
                        arrival(b, q).wait_recv()
                    use(b, q)

    for q in range(nq):
        for r in range(RG):
            out_ref[q * RG + r] = acc[q, :, r * 128 : r * 128 + tb]

    for copy in a_copies + d_copies + m_copies + x_copies:
        copy.wait_send()

    for q in range(nq):
        for side in range(2):
            for d in (1, 2):

                @pl.when(exists(away(side, d)))
                def _():
                    send(side, d, q).wait_send()

            @pl.when(forwards(side))
            def _():
                forward(side, q).wait_send()


def fused(nz, snapshot, level_factor, lon_factor, lat_factor):
    nk, ni, nj = snapshot.shape
    nr, ns, nt = level_factor.shape[1], lon_factor.shape[1], lat_factor.shape[1]
    half, sh, tb, lanes = nr // 2, ns // 2, nt // nz, RG * ni
    nq = half // RG
    dma = lambda *shape: pltpu.SemaphoreType.DMA(shape)
    vmem = pl.BlockSpec(memory_space=pltpu.VMEM)
    return pl.pallas_call(
        functools.partial(kernel, nz),
        out_shape=pltpu.VMEM((half, sh, tb), F32),
        in_specs=[pl.BlockSpec(memory_space=pltpu.HBM)] * 4,
        out_specs=vmem,
        scratch_shapes=[
            pltpu.VMEM((nk, ni, nj), BF16),
            pltpu.VMEM((nr, nk), BF16),
            pltpu.VMEM((ns, nj), BF16),
            dma(4),
            pltpu.VMEM((nr * IB, nk * IB), BF16),
            pltpu.VMEM((nz, lanes, RG * 128), BF16),
            pltpu.VMEM((half, ni // IB, IB, nj), F32),
            pltpu.VMEM((nq, ns, lanes), F32),
            pltpu.VMEM((nq, ns, lanes), F32),
            pltpu.VMEM((nq, ns, lanes), F32),
            pltpu.VMEM((nq, sh, lanes), BF16),
            pltpu.VMEM((nq, sh, lanes), BF16),
            pltpu.VMEM((nz, nq, sh, lanes), BF16),
            pltpu.VMEM((nz, ni, nt), BF16),
            pltpu.VMEM((8, 128), F32),
            pltpu.VMEM((8, 128), F32),
            pltpu.VMEM((nz, 8, 128), F32),
            pltpu.VMEM((nq, sh, RG * 128), F32),
            dma(nq), dma(nq), pltpu.SemaphoreType.DMA, pltpu.SemaphoreType.DMA, dma(nq), dma(nq),
            dma(nz - 1), dma(nz), dma(nz - 1), dma(nz), dma(2, 3, nq), dma(nz, nq),
        ],
        compiler_params=pltpu.CompilerParams(
            collective_id=0, has_side_effects=True, vmem_limit_bytes=58 * 2**20
        ),
    )(snapshot, level_factor.T, lon_factor.T, lat_factor)


def solution(mesh):
    in_specs = (P(("grp", "lev"), "lat", "lon"), P("lev", None), P("lon", None), P("lat", None))
    out_specs = P(("grp", "lev"), "lon", "lat")
    size = dict(mesh.shape)
    small = size["lev"] == 2 and size["lon"] == 2 and 1 < size["lat"] <= 4
    part = functools.partial(fused, size["lat"]) if small else body
    return jax.shard_map(part, mesh=mesh, in_specs=in_specs, out_specs=out_specs, check_vma=False)
```

```python
import functools

import jax
import jax.numpy as jnp
from jax import lax
from jax.experimental import pallas as pl
from jax.experimental.pallas import tpu as pltpu
from jax.sharding import PartitionSpec as P

MESH = pl.DeviceIdType.MESH
F32, BF16 = jnp.float32, jnp.bfloat16
TOP = 2.0**7
KNEE = 2.0**-6
RG = 8
IB = 16


def body(snapshot, level_factor, lon_factor, lat_factor):
    first = lax.psum_scatter(
        jnp.einsum("kij,kr->rij", snapshot, level_factor, preferred_element_type=jnp.float32),
        "lev",
        scatter_dimension=0,
        tiled=True,
    )
    lon_term = jnp.einsum(
        "rij,js->ris", first, lon_factor.astype(jnp.float32), precision=lax.Precision.HIGHEST
    )
    second = lax.psum_scatter(lon_term, "lon", scatter_dimension=2, tiled=True)
    lat_term = jnp.einsum(
        "ris,it->rst", second, lat_factor.astype(jnp.float32), precision=lax.Precision.HIGHEST
    )
    return lax.psum_scatter(lat_term, "lat", scatter_dimension=2, tiled=True)


def iota(shape, dim):
    return lax.broadcasted_iota(jnp.int32, shape, dim)


def dot(a, b):
    return jnp.dot(a, b, preferred_element_type=F32)


def dot_nt(a, b):
    return lax.dot_general(a, b, (((1,), (1,)), ((), ())), preferred_element_type=F32)


def encode(v, gain):
    w = v * gain
    small = jnp.abs(w) < KNEE
    w2 = w * w
    w4 = w2 * w2
    w8 = w4 * w4
    w16 = w8 * w8
    return jnp.where(small, w * (KNEE**15), jnp.where(w < 0, -w16, w16)).astype(BF16)


def decode(u, factor):
    u = u.astype(F32)
    size = jnp.abs(u)
    root = jnp.maximum(size, KNEE**16)
    root = lax.rsqrt(lax.rsqrt(root))
    root = lax.rsqrt(lax.rsqrt(root))
    return jnp.where(size < KNEE**16, u * (KNEE**-15), jnp.where(u < 0, -root, root)) * factor


def hi_lo(v):
    hi = v.astype(BF16)
    return hi, (v - hi.astype(F32)).astype(BF16)


def kernel(
    nz, x_hbm, l_hbm, o_hbm, a_hbm, out_ref,
    x_ref, l_ref, o_ref, in_sem, mx, w, f_ref, pown, psend, precv, xs, xr, g, ag, ptile, pr, mt, acc,
    d_send, d_recv, p_send, p_recv, x_send, x_recv, a_send, a_recv, m_send, m_recv, g_send, g_recv,
):
    nk, ni, nj = x_ref.shape
    nr = l_ref.shape[0]
    ns = o_ref.shape[0]
    half = nr // 2
    nq = half // RG
    sh = ns // 2
    nt = a_hbm.shape[1]
    tb = nt // nz
    lanes = RG * ni
    z = lax.axis_index("lat")
    x = lax.axis_index("lon")
    c = lax.axis_index("lev")
    mates = ({"lev": 1 - c}, {"lon": 1 - x})
    zpeers = [lax.rem(z + d, nz) for d in range(1, nz)]

    loads = [
        pltpu.make_async_copy(src, dst, in_sem.at[n])
        for n, (src, dst) in enumerate(((l_hbm, l_ref), (a_hbm, ag.at[z]), (x_hbm, x_ref), (o_hbm, o_ref)))
    ]
    for load in loads:
        load.start()
    barrier = pltpu.get_barrier_semaphore()
    for mate in mates:
        pl.semaphore_signal(barrier, inc=1, device_id=mate, device_id_type=MESH)
    for peer in zpeers:
        pl.semaphore_signal(barrier, inc=1, device_id={"lat": peer}, device_id_type=MESH)

    def remote(src, dst, ss, rs, dev):
        return pltpu.make_async_remote_copy(
            src_ref=src, dst_ref=dst, send_sem=ss, recv_sem=rs, device_id=dev, device_id_type=MESH
        )

    rows, cols = nr * IB, nk * IB
    spread_r = (iota((rows, nr), 0) // IB == iota((rows, nr), 1)).astype(BF16)
    spread_k = (iota((nk, cols), 1) // IB == iota((nk, cols), 0)).astype(BF16)
    same = (iota((IB, 128), 0) == iota((IB, 128), 1) % IB).astype(F32)
    loads[0].wait()
    lr = dot(spread_r, l_ref[...]).astype(BF16)
    for j in range(cols // 128):
        spread = dot(lr, spread_k[:, j * 128 : (j + 1) * 128]).reshape(nr, IB, 128) * same
        mx[:, j * 128 : (j + 1) * 128] = spread.reshape(rows, 128).astype(BF16)

    loads[1].wait()
    pl.semaphore_wait(barrier, 2 + nz - 1)
    a_copies = [
        remote(ag.at[z], ag.at[z], a_send.at[d], a_recv.at[z], {"lat": peer}) for d, peer in enumerate(zpeers)
    ]
    for copy in a_copies:
        copy.start()
    loads[2].wait()
    loads[3].wait()
    d_copies = []
    for side in range(2):
        h = (1 - c) if side == 0 else c
        rws = pl.ds(pl.multiple_of(h * (half * IB), half * IB), half * IB)
        part = mx[rws, :]
        for ib in range(ni // IB):
            blk = x_ref[:, ib * IB : (ib + 1) * IB, :].reshape(nk * IB, nj)
            f_ref[:, ib] = dot(part, blk).reshape(half, IB, nj)
        for q in range(nq):
            hi, lo = hi_lo(f_ref[q * RG : (q + 1) * RG].reshape(lanes, nj))
            p = dot_nt(o_ref[...], hi) + dot_nt(o_ref[...], lo)
            if side == 0:
                psend[q] = p
                copy = remote(psend.at[q], precv.at[q], d_send.at[q], d_recv.at[q], mates[0])
                copy.start()
                d_copies.append(copy)
            else:
                pown[q] = p
    most = jnp.zeros((8, 128), F32)
    for q in range(nq):
        d_copies[q].wait_recv()
        pown[q] = pown[q] + precv[q]
        m = jnp.max(jnp.abs(pown[q]).reshape(ns // 8, 8, lanes), axis=0)
        for j in range(lanes // 128):
            most = jnp.maximum(most, m[:, j * 128 : (j + 1) * 128])
    m_own = jnp.max(jnp.max(most, axis=0, keepdims=True), axis=1, keepdims=True)
    m_own = jnp.maximum(m_own, 1e-30)
    gain = TOP / m_own
    ptile[...] = jnp.broadcast_to(m_own, (8, 128))
    p_copy = remote(ptile, pr, p_send, p_recv, mates[1])
    p_copy.start()
    mine = pl.ds(pl.multiple_of(x * sh, sh), sh)
    theirs = pl.ds(pl.multiple_of((1 - x) * sh, sh), sh)
    x_copies = []
    for q in range(nq):
        xs[q] = encode(pown[q, theirs, :], gain)
        copy = remote(xs.at[q], xr.at[q], x_send.at[q], x_recv.at[q], mates[1])
        copy.start()
        x_copies.append(copy)

    w[...] = jnp.zeros(w.shape, BF16)
    for d, peer in enumerate(zpeers):
        remote(ag.at[z], ag.at[peer], a_send.at[d], a_recv.at[peer], {"lat": peer}).wait_recv()
    pick = iota((nt, 128), 1)
    pick = ((iota((nt, 128), 0) == pick + z * tb) & (pick < tb)).astype(BF16)
    for b in range(nz):
        own_t = dot(ag[b], pick).astype(BF16)
        for r in range(RG):
            w[b, r * ni : (r + 1) * ni, r * 128 : (r + 1) * 128] = own_t

    p_copy.wait()
    m_x = pr[0:1, 0:1]
    m = m_own + m_x
    mt[z] = jnp.broadcast_to(m, (8, 128))
    m_copies = [
        remote(mt.at[z], mt.at[z], m_send.at[d], m_recv.at[z], {"lat": peer}) for d, peer in enumerate(zpeers)
    ]
    for copy in m_copies:
        copy.start()
    gain, factor = TOP / m, m_x * (1 / TOP)

    def away(side, d):
        return z + d if side == 0 else z - d

    def exists(b):
        return (b >= 0) & (b < nz)

    def send(side, d, q):
        to = away(side, d)
        return remote(g.at[z, q], g.at[z, q], g_send.at[side, d - 1, q], g_recv.at[z, q], {"lat": to})

    def forward(side, q):
        b, to = away(1 - side, 2), away(side, 1)
        return remote(g.at[b, q], g.at[b, q], g_send.at[side, 2, q], g_recv.at[b, q], {"lat": to})

    def forwards(side):
        return exists(away(1 - side, 2)) & exists(away(side, 1))

    def arrival(b, q):
        return remote(g.at[z, q], g.at[b, q], g_send.at[0, 0, q], g_recv.at[b, q], {"lat": zpeers[0]})

    for q in range(nq):
        x_copies[q].wait_recv()
        val = pown[q, mine, :] + decode(xr[q], factor)
        g[z, q] = encode(val, gain)
        for d in (2, 1):
            for side in range(2):

                @pl.when(exists(away(side, d)))
                def _():
                    send(side, d, q).start()

    def use(b, q, own=False):
        hi, lo = hi_lo(decode(g[b, q], mt[b][0:1, 0:1] * (1 / TOP)))
        both = dot(jnp.concatenate([hi, lo], axis=0), w[b])
        acc[q] = both[:sh] + both[sh:] + (0.0 if own else acc[q])

    for q in range(nq):
        use(z, q, own=True)
    for d, peer in enumerate(zpeers):
        remote(mt.at[z], mt.at[peer], m_send.at[d], m_recv.at[peer], {"lat": peer}).wait_recv()

    for q in range(nq):
        for side in range(2):

            @pl.when(exists(away(1 - side, 2)))
            def _():
                arrival(away(1 - side, 2), q).wait_recv()

                @pl.when(forwards(side))
                def _():
                    forward(side, q).start()

        for side in range(2):
            b = away(side, 1)

            @pl.when(exists(b))
            def _():
                arrival(b, q).wait_recv()
                use(b, q)

        for side in range(2):
            b = away(side, 2)

            @pl.when(exists(b))
            def _():
                use(b, q)

    for d in range(3, nz):

        @pl.loop(0, nq)
        def _(q):
            for side in range(2):
                b = away(side, d)

                @pl.when(exists(b))
                def _():
                    arrival(b, q).wait_recv()
                    use(b, q)

    for q in range(nq):
        for r in range(RG):
            out_ref[q * RG + r] = acc[q, :, r * 128 : r * 128 + tb]

    for copy in a_copies + d_copies + m_copies + x_copies:
        copy.wait_send()

    for q in range(nq):
        for side in range(2):
            for d in (1, 2):

                @pl.when(exists(away(side, d)))
                def _():
                    send(side, d, q).wait_send()

            @pl.when(forwards(side))
            def _():
                forward(side, q).wait_send()


def fused(nz, snapshot, level_factor, lon_factor, lat_factor):
    nk, ni, nj = snapshot.shape
    nr, ns, nt = level_factor.shape[1], lon_factor.shape[1], lat_factor.shape[1]
    half, sh, tb, lanes = nr // 2, ns // 2, nt // nz, RG * ni
    nq = half // RG
    dma = lambda *shape: pltpu.SemaphoreType.DMA(shape)
    vmem = pl.BlockSpec(memory_space=pltpu.VMEM)
    return pl.pallas_call(
        functools.partial(kernel, nz),
        out_shape=pltpu.VMEM((half, sh, tb), F32),
        in_specs=[pl.BlockSpec(memory_space=pltpu.HBM)] * 4,
        out_specs=vmem,
        scratch_shapes=[
            pltpu.VMEM((nk, ni, nj), BF16),
            pltpu.VMEM((nr, nk), BF16),
            pltpu.VMEM((ns, nj), BF16),
            dma(4),
            pltpu.VMEM((nr * IB, nk * IB), BF16),
            pltpu.VMEM((nz, lanes, RG * 128), BF16),
            pltpu.VMEM((half, ni // IB, IB, nj), F32),
            pltpu.VMEM((nq, ns, lanes), F32),
            pltpu.VMEM((nq, ns, lanes), F32),
            pltpu.VMEM((nq, ns, lanes), F32),
            pltpu.VMEM((nq, sh, lanes), BF16),
            pltpu.VMEM((nq, sh, lanes), BF16),
            pltpu.VMEM((nz, nq, sh, lanes), BF16),
            pltpu.VMEM((nz, ni, nt), BF16),
            pltpu.VMEM((8, 128), F32),
            pltpu.VMEM((8, 128), F32),
            pltpu.VMEM((nz, 8, 128), F32),
            pltpu.VMEM((nq, sh, RG * 128), F32),
            dma(nq), dma(nq), pltpu.SemaphoreType.DMA, pltpu.SemaphoreType.DMA, dma(nq), dma(nq),
            dma(nz - 1), dma(nz), dma(nz - 1), dma(nz), dma(2, 3, nq), dma(nz, nq),
        ],
        compiler_params=pltpu.CompilerParams(
            collective_id=0, has_side_effects=True, vmem_limit_bytes=58 * 2**20
        ),
    )(snapshot, level_factor.T, lon_factor.T, lat_factor)


def solution(mesh):
    in_specs = (P(("grp", "lev"), "lat", "lon"), P("lev", None), P("lon", None), P("lat", None))
    out_specs = P(("grp", "lev"), "lon", "lat")
    size = dict(mesh.shape)
    small = size["lev"] == 2 and size["lon"] == 2 and 1 < size["lat"] <= 4
    part = functools.partial(fused, size["lat"]) if small else body
    return jax.shard_map(part, mesh=mesh, in_specs=in_specs, out_specs=out_specs, check_vma=False)
```
